32 devices in a mesh: row: 4 (over y, x), col: 4 (over z), depth: 2 (over core).
Axes of the slice: x: 2, y: 2, z: 4, core: 2. Of those that a mesh axis runs over, the one named last changes fastest.
Arguments:
- amplitude: float32 [100, 512, 512], P('row', 'depth', 'col'), may hold values from -6 to 6
- integral: float32 [512, 100, 2048], P('depth', None, 'col'), may hold values from -0.02734375 to 0.02734375
Outputs:
- cycle_term: float32 [512, 2048], P(('row', 'depth'), 'col')
The draws below stay inside these ranges and needn't reach their ends.
All inputs are finite; a program needn't handle non-finite values.
Results may differ from the reference program's by a relative error of at most 0.00011.
Values sent between devices are 32-bit elements; how exact they have to be, the bound alone decides.
No kernel may reach another device: no remote copies, remote signals or barrier semaphores. Data moves between devices by JAX's collectives and lax.ppermute only.
A program may use at most 128 MiB of HBM per device.

```python
import jax
import jax.numpy as jnp
from jax import lax

O = 100
VC = 512
ROWS = 512
COLS = 2048


def levels(stream_key, extent, split, low, high):
    factor_of = 1.0
    for position, blocks in split:
        draws = jax.random.uniform(jax.random.fold_in(jax.random.fold_in(stream_key, 6), position), (blocks,), jnp.float32, low / len(split), high / len(split))
        factor_of = factor_of * jnp.repeat(jnp.exp(draws), extent[position] // blocks).reshape((-1,) + (1,) * (len(extent) - 1 - position))
    return factor_of


def scatter_about(key, shape, width, reach, cuts=(), kind=jnp.bfloat16):
    level = levels(key, shape, cuts, -0.22, 0.18) if cuts else 1.0
    entries = jax.random.normal(key, shape, jnp.float32) * width * level
    return jnp.minimum(jnp.maximum(entries, -reach), reach).astype(kind)


def setup_inputs(seed: int = 0) -> dict:
    seeds = jax.random.split(jax.random.key(seed), 3)
    amplitude = scatter_about(seeds[0], (O, VC, ROWS), 1.0, 6.0, ((0, 4), (1, 2), (2, 4)), jnp.float32)
    integral = scatter_about(seeds[1], (VC, O, COLS), (VC * O) ** -0.5, 0.02734375, ((0, 2), (2, 4)), jnp.float32)
    return dict(amplitude=amplitude, integral=integral)


def reference(amplitude, integral):
    return jnp.einsum("kcm,ckn->mn", amplitude, integral, precision=lax.Precision.HIGHEST, preferred_element_type=jnp.float32)
```

```python
import jax
import jax.numpy as jnp
from jax import lax
from jax.sharding import PartitionSpec as P


def shards(amplitude, integral):
    ko = amplitude.shape[0]
    own = lax.dynamic_slice_in_dim(integral, lax.axis_index("row") * ko, ko, axis=1)
    product = jnp.einsum(
        "kcm,ckn->mn",
        lax.all_gather(amplitude, "col", axis=2, tiled=True),
        own,
        precision=lax.Precision.HIGH,
        preferred_element_type=jnp.float32,
    )
    return lax.psum_scatter(product, ("row", "depth"), scatter_dimension=0, tiled=True)


def solution(mesh):
    return jax.shard_map(
        shards,
        mesh=mesh,
        in_specs=(P("row", "depth", "col"), P("depth", None, "col")),
        out_specs=P(("row", "depth"), "col"),
        check_vma=False,
    )
```

```python
import jax
import jax.numpy as jnp
from jax import lax
from jax.sharding import PartitionSpec as P

LINE = 4


def after(value, *earlier):
    return lax.optimization_barrier((value,) + earlier)[0]


def bounds(start, stop, size):
    return [(k, min(k + size, stop)) for k in range(start, stop, size)]


def shards(amplitude, integral, rows, cols, layers):
    ko = amplitude.shape[0]
    group = cols // LINE
    row, col, layer = (lax.axis_index(name) for name in ("row", "col", "depth"))
    if group > 1:
        groups = [[z * group + lane for lane in range(group)] for z in range(LINE)]
        amplitude = lax.all_gather(amplitude, "col", axis=2, axis_index_groups=groups, tiled=True)
    place = col // group
    block, width = amplitude.shape[2], integral.shape[2]

    def hop(pairs):
        lanes = [(a * group + lane, b * group + lane) for a, b in pairs for lane in range(group)]
        return lambda value: lax.ppermute(value, "col", lanes)

    inward, across, outward = hop([(0, 1), (3, 2)]), hop([(1, 2), (2, 1)]), hop([(1, 0), (2, 3)])

    lent = round(ko * 2 * block / (3 * block + width))
    main = bounds(0, ko - lent, 3)
    extra = [(ko - lent, ko)]
    pieces = bounds(ko - lent, ko, 1)

    def weights(k0, k1):
        return lax.dynamic_slice_in_dim(integral, row * ko + k0, k1 - k0, axis=1)

    own = {c: amplitude[c[0] : c[1]] for c in main + extra}
    same_in, far_inner, far_end = {}, {}, {}
    out_same, out_inner, out_end, lent_weights = {}, {}, {}, {}

    sends = {"in": [], "across": [], "out": []}
    split = len(pieces) * 2 // 3
    sends["in"] += [(same_in, c, own, inward) for c in extra]
    sends["in"] += [(lent_weights, c, None, inward) for c in pieces[:split]]
    sends["in"] += [(same_in, c, own, inward) for c in main]
    sends["in"] += [(lent_weights, c, None, inward) for c in pieces[split:]]
    sends["across"] += [(far_inner, c, own, across) for c in main + extra]
    sends["across"] += [(far_end, c, same_in, across) for c in extra + main]
    sends["out"] += [(out_same, c, own, outward) for c in main]
    sends["out"] += [(out_inner, c, far_inner, outward) for c in main]
    sends["out"] += [(out_end, c, far_end, outward) for c in main]

    clock = dict.fromkeys(sends, 0)
    arrived = {name: [] for name in sends}
    while any(sends.values()):
        ready = [n for n in sends if sends[n] and (sends[n][0][2] is None or sends[n][0][1] in sends[n][0][2])]
        name = min(ready, key=lambda n: clock[n])
        into, c, source, move = sends[name].pop(0)
        value = weights(*c) if source is None else source[c]
        if len(arrived[name]) >= 2:
            value = after(value, arrived[name][-2])
        into[c] = move(value)
        arrived[name].append(into[c])
        clock[name] += (c[1] - c[0]) * (width / block if source is None else 1)

    def product(left, right):
        return jnp.einsum(
            "kcm,ckn->mn", left, right, precision=lax.Precision.HIGH, preferred_element_type=jnp.float32
        )

    slots = [0.0] * 4
    for c in main + extra:
        held = [own[c], same_in[c], far_inner[c], far_end[c]]
        if c in out_same:
            held = [held[0], held[1] + out_same[c], held[2] + out_inner[c], held[3] + out_end[c]]
        for s in range(4):
            slots[s] = slots[s] + product(held[s], weights(*c))

    loan = [0.0] * 4
    for k0, k1 in pieces:
        for s, held in ((1, own), (2, far_inner), (3, far_end)):
            base = extra[0][0]
            loan[s] = loan[s] + product(held[extra[0]][k0 - base : k1 - base], lent_weights[(k0, k1)])
    loan[0] = jnp.zeros_like(loan[1])

    table = jnp.array([[0, 1, 2, 3], [1, 0, 2, 3], [3, 2, 0, 1], [3, 2, 1, 0]], jnp.int32)

    def reduce_rows(blocks, where):
        halves = jnp.stack(blocks).reshape(4, layers, block // layers, width)
        if layers == 2:
            away = lax.dynamic_index_in_dim(halves, 1 - layer, 1, keepdims=False)
            mine = lax.dynamic_index_in_dim(halves, layer, 1, keepdims=False)
            mine = mine + lax.ppermute(away, "depth", [(0, 1), (1, 0)])
        else:
            mine = lax.psum_scatter(halves, "depth", scatter_dimension=1, tiled=False)
        total = lax.dynamic_index_in_dim(mine, table[where, row], 0, keepdims=False)
        for t in range(1, 4):
            part = lax.dynamic_index_in_dim(mine, table[where, row ^ t], 0, keepdims=False)
            total = total + lax.ppermute(part, "row", [(r, r ^ t) for r in range(4)])
        return total

    returned = outward(reduce_rows(loan, place ^ 1))
    return reduce_rows(slots, place) + returned


def solution(mesh):
    rows, cols, layers = (mesh.shape[name] for name in ("row", "col", "depth"))
    return jax.shard_map(
        lambda amplitude, integral: shards(amplitude, integral, rows, cols, layers),
        mesh=mesh,
        in_specs=(P("row", "depth", "col"), P("depth", None, "col")),
        out_specs=P(("row", "depth"), "col"),
        check_vma=False,
    )
```

```python
import functools

import jax
import jax.numpy as jnp
from jax import lax
from jax.experimental import pallas as pl
from jax.experimental.pallas import tpu as pltpu
from jax.sharding import PartitionSpec as P

LINE = 4


def after(value, *earlier):
    return lax.optimization_barrier((value,) + earlier)[0]


def bounds(start, *sizes):
    ends = [start + sum(sizes[: i + 1]) for i in range(len(sizes))]
    return [(stop - size, stop) for stop, size in zip(ends, sizes) if size > 0]


def thirds(count):
    return count - 2 * (count // 3), count // 3, count // 3


def parts(value):
    high = value.astype(jnp.bfloat16)
    return high, (value - high.astype(jnp.float32)).astype(jnp.bfloat16)


def contract_kernel(terms, first, offset_ref, *refs):
    del offset_ref
    out_ref = refs[-1]
    weight_ref = refs[sum(terms)]

    @pl.when(pl.program_id(0) == 0)
    def _():
        out_ref[...] = jnp.zeros_like(out_ref) if first else refs[sum(terms) + 1][...]

    highs, lows, at = [], [], 0
    for n in terms:
        value = refs[at][0]
        for ref in refs[at + 1 : at + n]:
            value = value + ref[0]
        at += n
        high, low = parts(value)
        highs.append(high)
        lows.append(low)
    high, low = parts(weight_ref[0])
    highs = jnp.concatenate(highs, axis=1)
    lows = jnp.concatenate(lows, axis=1)
    left = jnp.concatenate([highs, highs, lows], axis=0)
    right = jnp.concatenate([high, low, high], axis=0)
    product = lax.dot_general(left, right, (((0,), (0,)), ((), ())), preferred_element_type=jnp.float32)
    out_ref[...] += product.reshape(out_ref.shape)


def contract(slots, weights, offset, total):
    terms = [len(slot) for slot in slots]
    steps, depth, block = slots[0][0].shape
    width = weights.shape[2]
    shape = (len(slots), block, width)
    whole = pl.BlockSpec(shape, lambda i, o: (0, 0, 0))
    in_specs = [pl.BlockSpec((1, depth, block), lambda i, o: (i, 0, 0))] * sum(terms)
    in_specs.append(pl.BlockSpec((1, depth, width), lambda i, o: (o[0] + i, 0, 0)))
    operands = [a for slot in slots for a in slot] + [weights]
    aliases = {}
    if total is not None:
        in_specs.append(whole)
        aliases = {len(operands) + 1: 0}
        operands.append(total)
    return pl.pallas_call(
        functools.partial(contract_kernel, terms, total is None),
        out_shape=jax.ShapeDtypeStruct(shape, jnp.float32),
        grid_spec=pltpu.PrefetchScalarGridSpec(
            num_scalar_prefetch=1, grid=(steps,), in_specs=in_specs, out_specs=whole
        ),
        input_output_aliases=aliases,
        compiler_params=pltpu.CompilerParams(vmem_limit_bytes=40 << 20),
        cost_estimate=pl.CostEstimate(
            flops=6 * steps * depth * len(slots) * block * width,
            bytes_accessed=4 * (steps * depth * (width + sum(terms) * block) + 2 * len(slots) * block * width),
            transcendentals=0,
        ),
    )(jnp.reshape(offset, (1,)).astype(jnp.int32), *operands)


def shards(amplitude, integral, rows, cols, layers):
    ko = amplitude.shape[0]
    group = cols // LINE
    row, col, layer = (lax.axis_index(name) for name in ("row", "col", "depth"))
    if group > 1:
        groups = [[z * group + lane for lane in range(group)] for z in range(LINE)]
        amplitude = lax.all_gather(amplitude, "col", axis=2, axis_index_groups=groups, tiled=True)
    place = col // group
    block, width = amplitude.shape[2], integral.shape[2]
    integral = jnp.transpose(integral, (1, 0, 2))

    def hop(pairs):
        lanes = [(a * group + lane, b * group + lane) for a, b in pairs for lane in range(group)]
        return lambda value: lax.ppermute(value, "col", lanes)

    inward, across, outward = hop([(0, 1), (3, 2)]), hop([(1, 2), (2, 1)]), hop([(1, 0), (2, 3)])

    lent = round(ko * 2 * block / (3 * block + width))
    base = ko - lent
    main = bounds(0, *thirds(base))
    extra = (base, ko)
    sizes = [lent // 4 + (i < lent % 4) for i in range(4)]
    pieces = bounds(base, *sizes)

    own, same_in, far_inner, far_end = {}, {}, {}, {}
    out_same, out_inner, out_end, lent_weights = {}, {}, {}, {}
    last = main[-1]
    tail = bounds(last[0], last[1] - last[0] - (last[1] - last[0]) // 3, (last[1] - last[0]) // 3)

    sends = {"in": [], "across": [], "out": []}
    early = len(pieces) // 2
    sends["in"] += [(lent_weights, c, None, inward) for c in pieces[:early]]
    sends["in"] += [(same_in, c, own, inward) for c in main + [extra]]
    sends["in"] += [(lent_weights, c, None, inward) for c in pieces[early:]]
    sends["across"] += [(far_inner, c, own, across) for c in main + [extra]]
    sends["across"] += [(far_end, c, same_in, across) for c in main + [extra]]
    sends["out"] += [(out_same, c, own, outward) for c in main]
    sends["out"] += [(out_inner, c, far_inner, outward) for c in main]
    sends["out"] += [(out_end, c, far_end, outward) for c in main[:-1] + tail]

    def find(table, c):
        for (k0, k1), value in table.items():
            if k0 <= c[0] and c[1] <= k1:
                return value if (k0, k1) == c else value[c[0] - k0 : c[1] - k0]
        return None

    clock = dict.fromkeys(sends, 0)
    arrived = {name: [] for name in sends}
    newest = None
    while any(sends.values()):
        for c in main + [extra]:
            if c not in own and (newest is not None or c == main[0]):
                own[c] = (amplitude if newest is None else after(amplitude, newest))[c[0] : c[1]]
                break
        ready = [
            n
            for n in sends
            if sends[n] and (sends[n][0][2] is None or find(sends[n][0][2], sends[n][0][1]) is not None)
        ]
        name = min(ready, key=lambda n: (clock[n], n != "out"))
        into, c, source, move = sends[name].pop(0)
        if source is None:
            value = lax.dynamic_slice_in_dim(integral, row * ko + c[0], c[1] - c[0], axis=0)
        else:
            value = find(source, c)
        if len(arrived[name]) >= 2:
            value = after(value, arrived[name][-2])
        into[c] = newest = move(value)
        arrived[name].append(newest)
        clock[name] += (c[1] - c[0]) * (width / block if source is None else 1)

    near, far = None, None
    for c in main:
        near = contract([[own[c]], [same_in[c], out_same[c]], [far_inner[c], out_inner[c]]], integral, row * ko + c[0], near)
    near = contract([[own[extra]], [same_in[extra]], [far_inner[extra]]], integral, row * ko + base, near)
    for c in main[:-1] + tail:
        far = contract([[find(far_end, c), out_end[c]]], integral, row * ko + c[0], far)
    far = contract([[far_end[extra]]], integral, row * ko + base, far)

    loan = None
    for c in pieces:
        loan = contract(
            [[find(held, c)] for held in (own, far_inner, far_end)], lent_weights[c], jnp.int32(0), loan
        )

    table = jnp.array([[0, 1, 2, 3], [1, 0, 2, 3], [3, 2, 0, 1], [3, 2, 1, 0]], jnp.int32)

    def reduce_rows(blocks, where):
        halves = blocks.reshape(4, layers, block // layers, width)
        if layers == 2:
            away = lax.dynamic_index_in_dim(halves, 1 - layer, 1, keepdims=False)
            mine = lax.dynamic_index_in_dim(halves, layer, 1, keepdims=False)
            mine = mine + lax.ppermute(away, "depth", [(0, 1), (1, 0)])
        else:
            mine = lax.psum_scatter(halves, "depth", scatter_dimension=1, tiled=False)
        total = lax.dynamic_index_in_dim(mine, table[where, row], 0, keepdims=False)
        for t in range(1, 4):
            part = lax.dynamic_index_in_dim(mine, table[where, row ^ t], 0, keepdims=False)
            total = total + lax.ppermute(part, "row", [(r, r ^ t) for r in range(4)])
        return total

    returned = outward(reduce_rows(jnp.concatenate([jnp.zeros_like(far), loan]), place ^ 1))
    return reduce_rows(jnp.concatenate([near, far]), place) + returned


def solution(mesh):
    rows, cols, layers = (mesh.shape[name] for name in ("row", "col", "depth"))
    return jax.shard_map(
        lambda amplitude, integral: shards(amplitude, integral, rows, cols, layers),
        mesh=mesh,
        in_specs=(P("row", "depth", "col"), P("depth", None, "col")),
        out_specs=P(("row", "depth"), "col"),
        check_vma=False,
    )
```

```python
import functools

import jax
import jax.numpy as jnp
from jax import lax
from jax.experimental import pallas as pl
from jax.experimental.pallas import tpu as pltpu
from jax.sharding import PartitionSpec as P

LINE = 4


def after(value, *earlier):
    return lax.optimization_barrier((value,) + earlier)[0]


def bounds(start, *sizes):
    ends = [start + sum(sizes[: i + 1]) for i in range(len(sizes))]
    return [(stop - size, stop) for stop, size in zip(ends, sizes) if size > 0]


def parts(value):
    high = value.astype(jnp.bfloat16)
    return high, (value - high.astype(jnp.float32)).astype(jnp.bfloat16)


def contract_kernel(terms, per, first, offset_ref, *refs):
    del offset_ref
    out_ref = refs[-1]
    weight_refs = refs[sum(terms) : sum(terms) + per]

    @pl.when(pl.program_id(0) == 0)
    def _():
        out_ref[...] = jnp.zeros_like(out_ref) if first else refs[sum(terms) + per][...]

    left, right = [], []
    for j in range(per):
        highs, lows, at = [], [], 0
        for n in terms:
            value = refs[at][j]
            for ref in refs[at + 1 : at + n]:
                value = value + ref[j]
            at += n
            high, low = parts(value)
            highs.append(high)
            lows.append(low)
        highs = jnp.concatenate(highs, axis=1)
        left += [highs, highs, jnp.concatenate(lows, axis=1)]
        high, low = parts(weight_refs[j][0])
        right += [high, low, high]
    product = lax.dot_general(
        jnp.concatenate(left, axis=0),
        jnp.concatenate(right, axis=0),
        (((0,), (0,)), ((), ())),
        preferred_element_type=jnp.float32,
    )
    out_ref[...] += product.reshape(out_ref.shape)


def contract(slots, weights, offset, total):
    terms = [len(slot) for slot in slots]
    steps, depth, block = slots[0][0].shape
    width = weights.shape[2]
    per = max(n for n in (1, 2, 3) if steps % n == 0)
    shape = (len(slots), block, width)
    whole = pl.BlockSpec(shape, lambda i, o: (0, 0, 0))
    in_specs = [pl.BlockSpec((per, depth, block), lambda i, o: (i, 0, 0))] * sum(terms)
    for j in range(per):
        in_specs.append(pl.BlockSpec((1, depth, width), lambda i, o, j=j: (o[0] + per * i + j, 0, 0)))
    operands = [a for slot in slots for a in slot] + [weights] * per
    aliases = {}
    if total is not None:
        in_specs.append(whole)
        aliases = {len(operands) + 1: 0}
        operands.append(total)
    return pl.pallas_call(
        functools.partial(contract_kernel, terms, per, total is None),
        out_shape=jax.ShapeDtypeStruct(shape, jnp.float32),
        grid_spec=pltpu.PrefetchScalarGridSpec(
            num_scalar_prefetch=1, grid=(steps // per,), in_specs=in_specs, out_specs=whole
        ),
        input_output_aliases=aliases,
        compiler_params=pltpu.CompilerParams(vmem_limit_bytes=40 << 20),
        cost_estimate=pl.CostEstimate(
            flops=6 * steps * depth * len(slots) * block * width,
            bytes_accessed=4 * (steps * depth * (width + sum(terms) * block) + 2 * len(slots) * block * width),
            transcendentals=0,
        ),
    )(jnp.reshape(offset, (1,)).astype(jnp.int32), *operands)


def shards(amplitude, integral, rows, cols, layers):
    ko = amplitude.shape[0]
    group = cols // LINE
    row, col, layer = (lax.axis_index(name) for name in ("row", "col", "depth"))
    if group > 1:
        groups = [[z * group + lane for lane in range(group)] for z in range(LINE)]
        amplitude = lax.all_gather(amplitude, "col", axis=2, axis_index_groups=groups, tiled=True)
    place = col // group
    block, width = amplitude.shape[2], integral.shape[2]
    integral = jnp.transpose(integral, (1, 0, 2))

    def hop(pairs):
        lanes = [(a * group + lane, b * group + lane) for a, b in pairs for lane in range(group)]
        return lambda value: lax.ppermute(value, "col", lanes)

    inward, across, outward = hop([(0, 1), (3, 2)]), hop([(1, 2), (2, 1)]), hop([(1, 0), (2, 3)])

    lent = round(ko * 2 * block / (3 * block + width))
    base = ko - lent
    main = bounds(0, base - base // 2, base // 2)
    extra = (base, ko)
    sizes = [lent // 4 + (i + lent % 4 >= 4) for i in range(4)]
    pieces = bounds(base, sizes[1], sizes[0], *sizes[2:])
    last = main[-1]
    size = last[1] - last[0]
    tail = bounds(last[0], size - size // 3, size // 3)

    own = {main[0]: amplitude[: main[0][1]]}
    later = after(amplitude, own[main[0]])
    for c in main[1:] + [extra]:
        own[c] = later[c[0] : c[1]]
    same_in, far_inner, far_end = {}, {}, {}
    out_same, out_inner, out_end, lent_weights = {}, {}, {}, {}

    sends = {"out": [], "across": [], "in": []}
    early = len(pieces) // 2
    sends["in"] += [(lent_weights, c, None, inward) for c in pieces[:early]]
    sends["in"] += [(same_in, c, own, inward) for c in main + [extra]]
    sends["in"] += [(lent_weights, c, None, inward) for c in pieces[early:]]
    sends["across"] += [(far_inner, c, own, across) for c in main + [extra]]
    sends["across"] += [(far_end, c, same_in, across) for c in main + [extra]]
    sends["out"] += [(out_same, c, own, outward) for c in main]
    sends["out"] += [(out_inner, c, far_inner, outward) for c in main]
    sends["out"] += [(out_end, c, far_end, outward) for c in main[:-1] + tail]

    def find(table, c):
        for (k0, k1), value in table.items():
            if k0 <= c[0] and c[1] <= k1:
                return value if (k0, k1) == c else value[c[0] - k0 : c[1] - k0]
        return None

    clock = dict.fromkeys(sends, 0)
    arrived = {name: [] for name in sends}
    while any(sends.values()):
        ready = [n for n in sends if sends[n]]
        ready = [n for n in ready if sends[n][0][2] is None or find(sends[n][0][2], sends[n][0][1]) is not None]
        name = min(ready, key=lambda n: clock[n])
        into, c, source, move = sends[name].pop(0)
        if source is None:
            value = lax.dynamic_slice_in_dim(integral, row * ko + c[0], c[1] - c[0], axis=0)
        else:
            value = find(source, c)
        if len(arrived[name]) >= 2:
            value = after(value, arrived[name][-2])
        into[c] = move(value)
        arrived[name].append(into[c])
        clock[name] += (c[1] - c[0]) * (width / block if source is None else 1)

    near, far, loan = None, None, None
    for c in main:
        slots = [[own[c]], [same_in[c], out_same[c]], [far_inner[c], out_inner[c]]]
        near = contract(slots, integral, row * ko + c[0], near)
    near = contract([[own[extra]], [same_in[extra]], [far_inner[extra]]], integral, row * ko + base, near)
    for c in main[:-1] + [extra] + tail:
        slots = [[find(far_end, c)] + ([out_end[c]] if c in out_end else [])]
        far = contract(slots, integral, row * ko + c[0], far)
    for c in pieces:
        slots = [[find(held, c)] for held in (own, far_inner, far_end)]
        loan = contract(slots, lent_weights[c], jnp.int32(0), loan)

    def layer_sum(blocks):
        halves = blocks.reshape(blocks.shape[0], layers, block // layers, width)
        if layers != 2:
            return lax.psum_scatter(halves, "depth", scatter_dimension=1, tiled=False)
        away = lax.dynamic_index_in_dim(halves, 1 - layer, 1, keepdims=False)
        mine = lax.dynamic_index_in_dim(halves, layer, 1, keepdims=False)
        return mine + lax.ppermute(away, "depth", [(0, 1), (1, 0)])

    inner = jnp.logical_or(place == 1, place == 2).astype(jnp.int32)

    def row_sum(halves, swapped):
        def part(target):
            mirrored = jnp.where(place < 2, target, 3 - target)
            slot = mirrored ^ (swapped * (mirrored < 2).astype(jnp.int32))
            return lax.dynamic_index_in_dim(halves, slot, 0, keepdims=False)

        total = part(row)
        for t in range(1, 4):
            total = total + lax.ppermute(part(row ^ t), "row", [(r, r ^ t) for r in range(4)])
        return total

    near = layer_sum(near)
    loan = layer_sum(loan)
    returned = outward(row_sum(jnp.concatenate([jnp.zeros_like(loan[:1]), loan]), 0))
    return row_sum(jnp.concatenate([near, layer_sum(far)]), inner) + returned


def solution(mesh):
    rows, cols, layers = (mesh.shape[name] for name in ("row", "col", "depth"))
    return jax.shard_map(
        lambda amplitude, integral: shards(amplitude, integral, rows, cols, layers),
        mesh=mesh,
        in_specs=(P("row", "depth", "col"), P("depth", None, "col")),
        out_specs=P(("row", "depth"), "col"),
        check_vma=False,
    )
```

```python
import functools

import jax
import jax.numpy as jnp
from jax import lax
from jax.experimental import pallas as pl
from jax.experimental.pallas import tpu as pltpu
from jax.sharding import PartitionSpec as P

LINE = 4
HALVES = 2


def after(value, *earlier):
    return lax.optimization_barrier((value,) + earlier)[0]


def bounds(start, *sizes):
    ends = [start + sum(sizes[: i + 1]) for i in range(len(sizes))]
    return [(stop - size, stop) for stop, size in zip(ends, sizes) if size > 0]


def parts(value):
    high = value.astype(jnp.bfloat16)
    return high, (value - high.astype(jnp.float32)).astype(jnp.bfloat16)


def contract_kernel(terms, per, first, offset_ref, *refs):
    del offset_ref
    out_ref = refs[-1]
    weight_refs = refs[sum(terms) : sum(terms) + per]

    @pl.when(pl.program_id(0) == 0)
    def _():
        out_ref[...] = jnp.zeros_like(out_ref) if first else refs[sum(terms) + per][...]

    left, right = [], []
    for j in range(per):
        highs, lows, at = [], [], 0
        for n in terms:
            value = refs[at][j]
            for ref in refs[at + 1 : at + n]:
                value = value + ref[j]
            at += n
            high, low = parts(value)
            highs.append(high)
            lows.append(low)
        highs = jnp.concatenate(highs, axis=1)
        left += [highs, highs, jnp.concatenate(lows, axis=1)]
        high, low = parts(weight_refs[j][0])
        right += [high, low, high]
    product = lax.dot_general(
        jnp.concatenate(left, axis=0),
        jnp.concatenate(right, axis=0),
        (((0,), (0,)), ((), ())),
        preferred_element_type=jnp.float32,
    )
    out_ref[...] += product.reshape(out_ref.shape)


def contract_run(slots, weights, offset, total, start, per, steps):
    terms = [len(slot) for slot in slots]
    _, depth, block = slots[0][0].shape
    width = weights.shape[2]
    shape = (len(slots), block, width)
    whole = pl.BlockSpec(shape, lambda i, o: (0, 0, 0))
    in_specs = [pl.BlockSpec((per, depth, block), lambda i, o: (start // per + i, 0, 0))] * sum(terms)
    for j in range(per):
        in_specs.append(pl.BlockSpec((1, depth, width), lambda i, o, j=j: (o[0] + start + per * i + j, 0, 0)))
    operands = [a for slot in slots for a in slot] + [weights] * per
    aliases = {}
    if total is not None:
        in_specs.append(whole)
        aliases = {len(operands) + 1: 0}
        operands.append(total)
    units = steps * per * depth
    return pl.pallas_call(
        functools.partial(contract_kernel, terms, per, total is None),
        out_shape=jax.ShapeDtypeStruct(shape, jnp.float32),
        grid_spec=pltpu.PrefetchScalarGridSpec(
            num_scalar_prefetch=1, grid=(steps,), in_specs=in_specs, out_specs=whole
        ),
        input_output_aliases=aliases,
        compiler_params=pltpu.CompilerParams(vmem_limit_bytes=40 << 20),
        cost_estimate=pl.CostEstimate(
            flops=6 * units * len(slots) * block * width,
            bytes_accessed=4 * (units * (width + sum(terms) * block) + 2 * len(slots) * block * width),
            transcendentals=0,
        ),
    )(jnp.reshape(offset, (1,)).astype(jnp.int32), *operands)


def contract(slots, weights, offset, total):
    count = slots[0][0].shape[0]
    per = min(6, count)
    total = contract_run(slots, weights, offset, total, 0, per, count // per)
    left = count % per
    if left:
        total = contract_run(slots, weights, offset, total, count - left, 1, left)
    return total


def shards(amplitude, integral, rows, cols, layers):
    group = cols // LINE
    row, col, layer = (lax.axis_index(name) for name in ("row", "col", "depth"))
    if group > 1:
        groups = [[z * group + lane for lane in range(group)] for z in range(LINE)]
        amplitude = lax.all_gather(amplitude, "col", axis=2, axis_index_groups=groups, tiled=True)
    place = col // group
    block, width = amplitude.shape[2], integral.shape[2]
    integral = jnp.transpose(integral, (1, 0, 2)).reshape(-1, integral.shape[0] // HALVES, width)
    amplitude = amplitude.reshape(-1, amplitude.shape[1] // HALVES, block)
    ko = amplitude.shape[0]

    def hop(pairs):
        lanes = [(a * group + lane, b * group + lane) for a, b in pairs for lane in range(group)]
        return lambda value: lax.ppermute(value, "col", lanes)

    inward, across, outward = hop([(0, 1), (3, 2)]), hop([(1, 2), (2, 1)]), hop([(1, 0), (2, 3)])
    swap = hop([(0, 1), (1, 0), (2, 3), (3, 2)])

    lent = round(ko * 2 * block / (3 * block + width)) - 1
    base = ko - lent
    main = bounds(0, base - base // 2, base // 2)
    extra = (base, ko)
    pieces = bounds(base, *[lent // 5 + (i < lent % 5) for i in range(5)])
    ends = []
    for start, stop in main:
        cut = (stop - start) // 2 if not ends else (stop - start) // 3
        ends += bounds(start, stop - start - cut, cut)

    own = {main[0]: amplitude[: main[0][1]]}
    later = after(amplitude, own[main[0]])
    shift = after(row, own[main[0]]) * ko
    for c in main[1:] + [extra]:
        own[c] = later[c[0] : c[1]]
    same, far_inner, far_end, out_inner, out_end, lent_weights = {}, {}, {}, {}, {}, {}

    def find(table, c):
        for (k0, k1), value in table.items():
            if k0 <= c[0] and c[1] <= k1:
                return value if (k0, k1) == c else value[c[0] - k0 : c[1] - k0]
        return None

    done = {"out": [], "across": [], "in": []}

    def send(name, into, c, source, move):
        if source is None:
            value = lax.dynamic_slice_in_dim(integral, shift + c[0], c[1] - c[0], axis=0)
        else:
            value = find(source, c)
        if len(done[name]) >= 2:
            value = after(value, done[name][-2])
        into[c] = move(value)
        done[name].append(into[c])

    for c in main:
        send("out", same, c, own, swap)
        done["in"].append(same[c])
    for c in main + [extra]:
        send("across", far_inner, c, own, across)
    for c in main:
        send("out", out_inner, c, far_inner, outward)
    send("in", same, extra, own, inward)
    for c in main + [extra]:
        send("across", far_end, c, same, across)
    for c in ends:
        send("out", out_end, c, far_end, outward)
    for c in pieces:
        send("in", lent_weights, c, None, inward)

    near, far, loan = None, None, None
    for c in main:
        slots = [[own[c]], [same[c]], [far_inner[c], out_inner[c]]]
        near = contract(slots, integral, row * ko + c[0], near)
    near = contract([[own[extra]], [same[extra]], [far_inner[extra]]], integral, row * ko + base, near)
    for c in ends[:2] + [extra] + ends[2:]:
        slots = [[find(far_end, c)] + ([out_end[c]] if c in out_end else [])]
        far = contract(slots, integral, row * ko + c[0], far)
    for c in pieces:
        slots = [[find(held, c)] for held in (own, far_inner, far_end)]
        loan = contract(slots, lent_weights[c], jnp.int32(0), loan)

    def layer_sum(blocks):
        halves = blocks.reshape(blocks.shape[0], layers, block // layers, width)
        if layers != 2:
            return lax.psum_scatter(halves, "depth", scatter_dimension=1, tiled=False)
        away = lax.dynamic_index_in_dim(halves, 1 - layer, 1, keepdims=False)
        mine = lax.dynamic_index_in_dim(halves, layer, 1, keepdims=False)
        return mine + lax.ppermute(away, "depth", [(0, 1), (1, 0)])

    inner = jnp.logical_or(place == 1, place == 2).astype(jnp.int32)

    def row_sum(halves, swapped):
        def part(target):
            mirrored = jnp.where(place < 2, target, 3 - target)
            slot = mirrored ^ (swapped * (mirrored < 2).astype(jnp.int32))
            return lax.dynamic_index_in_dim(halves, slot, 0, keepdims=False)

        total = part(row)
        for t in range(1, 4):
            total = total + lax.ppermute(part(row ^ t), "row", [(r, r ^ t) for r in range(4)])
        return total

    near = layer_sum(near)
    loan = layer_sum(loan)
    returned = outward(row_sum(jnp.concatenate([jnp.zeros_like(loan[:1]), loan]), 0))
    return row_sum(jnp.concatenate([near, layer_sum(far)]), inner) + returned


def solution(mesh):
    rows, cols, layers = (mesh.shape[name] for name in ("row", "col", "depth"))
    return jax.shard_map(
        lambda amplitude, integral: shards(amplitude, integral, rows, cols, layers),
        mesh=mesh,
        in_specs=(P("row", "depth", "col"), P("depth", None, "col")),
        out_specs=P(("row", "depth"), "col"),
        check_vma=False,
    )
```

```python
import functools

import jax
import jax.numpy as jnp
from jax import lax
from jax.experimental import pallas as pl
from jax.experimental.pallas import tpu as pltpu
from jax.sharding import PartitionSpec as P

LINE = 4
HALVES = 2


def after(value, *earlier):
    return lax.optimization_barrier((value,) + earlier)[0]


def bounds(start, *sizes):
    ends = [start + sum(sizes[: i + 1]) for i in range(len(sizes))]
    return [(stop - size, stop) for stop, size in zip(ends, sizes) if size > 0]


def parts(value):
    high = value.astype(jnp.bfloat16)
    return high, (value - high.astype(jnp.float32)).astype(jnp.bfloat16)


def contract_kernel(terms, per, first, offset_ref, *refs):
    del offset_ref
    out_ref = refs[-1]
    weight_refs = refs[sum(terms) : sum(terms) + per]

    @pl.when(pl.program_id(0) == 0)
    def _():
        out_ref[...] = jnp.zeros_like(out_ref) if first else refs[sum(terms) + per][...]

    left, right = [], []
    for j in range(per):
        highs, lows, at = [], [], 0
        for n in terms:
            value = refs[at][j]
            for ref in refs[at + 1 : at + n]:
                value = value + ref[j]
            at += n
            high, low = parts(value)
            highs.append(high)
            lows.append(low)
        highs = jnp.concatenate(highs, axis=1)
        left += [highs, highs, jnp.concatenate(lows, axis=1)]
        high, low = parts(weight_refs[j][0])
        right += [high, low, high]
    product = lax.dot_general(
        jnp.concatenate(left, axis=0),
        jnp.concatenate(right, axis=0),
        (((0,), (0,)), ((), ())),
        preferred_element_type=jnp.float32,
    )
    out_ref[...] += product.reshape(out_ref.shape)


def contract_run(slots, weights, offset, total, start, per, steps):
    terms = [len(slot) for slot in slots]
    _, depth, block = slots[0][0].shape
    width = weights.shape[2]
    shape = (len(slots), block, width)
    whole = pl.BlockSpec(shape, lambda i, o: (0, 0, 0))
    in_specs = [pl.BlockSpec((per, depth, block), lambda i, o: (start // per + i, 0, 0))] * sum(terms)
    for j in range(per):
        in_specs.append(pl.BlockSpec((1, depth, width), lambda i, o, j=j: (o[0] + start + per * i + j, 0, 0)))
    operands = [a for slot in slots for a in slot] + [weights] * per
    aliases = {}
    if total is not None:
        in_specs.append(whole)
        aliases = {len(operands) + 1: 0}
        operands.append(total)
    return pl.pallas_call(
        functools.partial(contract_kernel, terms, per, total is None),
        out_shape=jax.ShapeDtypeStruct(shape, jnp.float32),
        grid_spec=pltpu.PrefetchScalarGridSpec(
            num_scalar_prefetch=1, grid=(steps,), in_specs=in_specs, out_specs=whole
        ),
        input_output_aliases=aliases,
        compiler_params=pltpu.CompilerParams(vmem_limit_bytes=40 << 20),
    )(jnp.reshape(offset, (1,)).astype(jnp.int32), *operands)


def contract(slots, weights, offset, total):
    count = slots[0][0].shape[0]
    per = min(6, count)
    total = contract_run(slots, weights, offset, total, 0, per, count // per)
    left = count % per
    if left:
        total = contract_run(slots, weights, offset, total, count - left, 1, left)
    return total


def shards(amplitude, integral, rows, cols, layers):
    group = cols // LINE
    row, col, layer = (lax.axis_index(name) for name in ("row", "col", "depth"))
    if group > 1:
        groups = [[z * group + lane for lane in range(group)] for z in range(LINE)]
        amplitude = lax.all_gather(amplitude, "col", axis=2, axis_index_groups=groups, tiled=True)
    place = col // group
    block, width = amplitude.shape[2], integral.shape[2]
    integral = jnp.transpose(integral, (1, 0, 2)).reshape(-1, integral.shape[0] // HALVES, width)
    amplitude = amplitude.reshape(-1, amplitude.shape[1] // HALVES, block)
    ko = amplitude.shape[0]

    def hop(pairs):
        lanes = [(a * group + lane, b * group + lane) for a, b in pairs for lane in range(group)]
        return lambda value: lax.ppermute(value, "col", lanes)

    inward, across, outward = hop([(0, 1), (3, 2)]), hop([(1, 2), (2, 1)]), hop([(1, 0), (2, 3)])
    swap = hop([(0, 1), (1, 0), (2, 3), (3, 2)])

    lent = round(ko * 2 * block / (3 * block + width)) - 1
    base = ko - lent
    main = bounds(0, base // 2, base - base // 2)
    extra = (base, ko)
    pieces = bounds(base, *[lent // 5 + (i < lent % 5) for i in range(5)])
    ends = []
    for start, stop in main:
        cut = (stop - start) // 2 if not ends else (stop - start) // 3
        ends += bounds(start, stop - start - cut, cut)

    own = {main[0]: amplitude[: main[0][1]]}
    later = after(amplitude, own[main[0]])
    shift = after(row, own[main[0]]) * ko
    for c in main[1:] + [extra]:
        own[c] = later[c[0] : c[1]]
    same, far_inner, far_end, out_inner, out_end, lent_weights = {}, {}, {}, {}, {}, {}

    def find(table, c):
        for (k0, k1), value in table.items():
            if k0 <= c[0] and c[1] <= k1:
                return value if (k0, k1) == c else value[c[0] - k0 : c[1] - k0]
        return None

    done = {"out": [], "across": [], "in": []}

    def send(name, into, c, source, move):
        if source is None:
            value = lax.dynamic_slice_in_dim(integral, shift + c[0], c[1] - c[0], axis=0)
        else:
            value = find(source, c)
        if len(done[name]) >= 2:
            value = after(value, done[name][-2])
        into[c] = move(value)
        done[name].append(into[c])

    for c in main:
        send("out", same, c, own, swap)
        done["in"].append(same[c])
    for c in main + [extra]:
        send("across", far_inner, c, own, across)
    for c in main:
        send("out", out_inner, c, far_inner, outward)
    send("in", same, extra, own, inward)
    for c in main + [extra]:
        send("across", far_end, c, same, across)
    for c in ends:
        send("out", out_end, c, far_end, outward)
    for c in pieces:
        send("in", lent_weights, c, None, inward)

    near, far, loan = None, None, None
    for c in main:
        slots = [[own[c]], [same[c]], [far_inner[c], out_inner[c]]]
        near = contract(slots, integral, row * ko + c[0], near)
    near = contract([[own[extra]], [same[extra]], [far_inner[extra]]], integral, row * ko + base, near)
    for c in ends[:2] + [extra] + ends[2:]:
        slots = [[find(far_end, c)] + ([out_end[c]] if c in out_end else [])]
        far = contract(slots, integral, row * ko + c[0], far)
    for c in pieces:
        slots = [[find(held, c)] for held in (own, far_inner, far_end)]
        loan = contract(slots, lent_weights[c], jnp.int32(0), loan)

    def layer_sum(blocks):
        halves = blocks.reshape(blocks.shape[0], layers, block // layers, width)
        if layers != 2:
            return lax.psum_scatter(halves, "depth", scatter_dimension=1, tiled=False)
        away = lax.dynamic_index_in_dim(halves, 1 - layer, 1, keepdims=False)
        mine = lax.dynamic_index_in_dim(halves, layer, 1, keepdims=False)
        return mine + lax.ppermute(away, "depth", [(0, 1), (1, 0)])

    inner = jnp.logical_or(place == 1, place == 2).astype(jnp.int32)

    def row_sum(halves, swapped):
        def part(target):
            mirrored = jnp.where(place < 2, target, 3 - target)
            slot = mirrored ^ (swapped * (mirrored < 2).astype(jnp.int32))
            return lax.dynamic_index_in_dim(halves, slot, 0, keepdims=False)

        total = part(row)
        for t in range(1, 4):
            total = total + lax.ppermute(part(row ^ t), "row", [(r, r ^ t) for r in range(4)])
        return total

    near = layer_sum(near)
    loan = layer_sum(loan)
    returned = outward(row_sum(jnp.concatenate([jnp.zeros_like(loan[:1]), loan]), 0))
    return row_sum(jnp.concatenate([near, layer_sum(far)]), inner) + returned


def solution(mesh):
    rows, cols, layers = (mesh.shape[name] for name in ("row", "col", "depth"))
    return jax.shard_map(
        lambda amplitude, integral: shards(amplitude, integral, rows, cols, layers),
        mesh=mesh,
        in_specs=(P("row", "depth", "col"), P("depth", None, "col")),
        out_specs=P(("row", "depth"), "col"),
        check_vma=False,
    )
```

```python
import functools

import jax
import jax.numpy as jnp
from jax import lax
from jax.experimental import pallas as pl
from jax.experimental.pallas import tpu as pltpu
from jax.sharding import PartitionSpec as P

LINE = 4
HALVES = 2


def after(value, *earlier):
    return lax.optimization_barrier((value,) + earlier)[0]


def bounds(start, *sizes):
    ends = [start + sum(sizes[: i + 1]) for i in range(len(sizes))]
    return [(stop - size, stop) for stop, size in zip(ends, sizes) if size > 0]


def parts(value):
    high = value.astype(jnp.bfloat16)
    return high, (value - high.astype(jnp.float32)).astype(jnp.bfloat16)


def contract_kernel(terms, per, first, offset_ref, *refs):
    del offset_ref
    out_ref = refs[-1]
    weight_refs = refs[sum(terms) : sum(terms) + per]

    @pl.when(pl.program_id(0) == 0)
    def _():
        out_ref[...] = jnp.zeros_like(out_ref) if first else refs[sum(terms) + per][...]

    left, right = [], []
    for j in range(per):
        highs, lows, at = [], [], 0
        for n in terms:
            value = refs[at][j]
            for ref in refs[at + 1 : at + n]:
                value = value + ref[j]
            at += n
            high, low = parts(value)
            highs.append(high)
            lows.append(low)
        highs = jnp.concatenate(highs, axis=1)
        left += [highs, highs, jnp.concatenate(lows, axis=1)]
        high, low = parts(weight_refs[j][0])
        right += [high, low, high]
    product = lax.dot_general(
        jnp.concatenate(left, axis=0),
        jnp.concatenate(right, axis=0),
        (((0,), (0,)), ((), ())),
        preferred_element_type=jnp.float32,
    )
    out_ref[...] += product.reshape(out_ref.shape)


def contract_run(slots, weights, offset, total, start, per, steps):
    terms = [len(slot) for slot in slots]
    _, depth, block = slots[0][0].shape
    width = weights.shape[2]
    shape = (len(slots), block, width)
    whole = pl.BlockSpec(shape, lambda i, o: (0, 0, 0))
    in_specs = [pl.BlockSpec((per, depth, block), lambda i, o: (start // per + i, 0, 0))] * sum(terms)
    for j in range(per):
        in_specs.append(pl.BlockSpec((1, depth, width), lambda i, o, j=j: (o[0] + start + per * i + j, 0, 0)))
    operands = [a for slot in slots for a in slot] + [weights] * per
    aliases = {}
    if total is not None:
        in_specs.append(whole)
        aliases = {len(operands) + 1: 0}
        operands.append(total)
    return pl.pallas_call(
        functools.partial(contract_kernel, terms, per, total is None),
        out_shape=jax.ShapeDtypeStruct(shape, jnp.float32),
        grid_spec=pltpu.PrefetchScalarGridSpec(
            num_scalar_prefetch=1, grid=(steps,), in_specs=in_specs, out_specs=whole
        ),
        input_output_aliases=aliases,
        compiler_params=pltpu.CompilerParams(vmem_limit_bytes=40 << 20),
    )(jnp.reshape(offset, (1,)).astype(jnp.int32), *operands)


def contract(slots, weights, offset, total):
    count = slots[0][0].shape[0]
    per = max(n for n in range(1, 7) if count % n == 0)
    if per < 3:
        per = min(6, count)
    total = contract_run(slots, weights, offset, total, 0, per, count // per)
    left = count % per
    if left:
        total = contract_run(slots, weights, offset, total, count - left, 1, left)
    return total


def shards(amplitude, integral, rows, cols, layers):
    group = cols // LINE
    row, col, layer = (lax.axis_index(name) for name in ("row", "col", "depth"))
    if group > 1:
        groups = [[z * group + lane for lane in range(group)] for z in range(LINE)]
        amplitude = lax.all_gather(amplitude, "col", axis=2, axis_index_groups=groups, tiled=True)
    place = col // group
    block, width = amplitude.shape[2], integral.shape[2]
    integral = jnp.transpose(integral, (1, 0, 2)).reshape(-1, integral.shape[0] // HALVES, width)
    amplitude = amplitude.reshape(-1, amplitude.shape[1] // HALVES, block)
    ko = amplitude.shape[0]

    def hop(pairs):
        lanes = [(a * group + lane, b * group + lane) for a, b in pairs for lane in range(group)]
        return lambda value: lax.ppermute(value, "col", lanes)

    inward, across, outward = hop([(0, 1), (3, 2)]), hop([(1, 2), (2, 1)]), hop([(1, 0), (2, 3)])
    swap = hop([(0, 1), (1, 0), (2, 3), (3, 2)])

    lent = round(ko * 2 * block / (3 * block + width)) - 1
    base = ko - lent
    main = bounds(0, base // 2, base - base // 2)
    extra = (base, ko)
    pieces = bounds(base, *[lent // 5 + (i < lent % 5) for i in range(5)])
    first, second = main
    half = (first[1] - first[0]) // 2
    third = (second[1] - second[0]) // 3
    heads = bounds(first[0], first[1] - first[0] - half, half)
    tails = bounds(second[0], second[1] - second[0] - third, third)

    own = {first: amplitude[: first[1]]}
    later = after(amplitude, own[first])
    shift = after(row, own[first]) * ko
    for c in [second, extra]:
        own[c] = later[c[0] : c[1]]
    same, far_inner, far_end, out_inner, out_end, lent_weights = {}, {}, {}, {}, {}, {}
    tables = {
        "own": own,
        "same": same,
        "far_inner": far_inner,
        "far_end": far_end,
        "out_inner": out_inner,
        "out_end": out_end,
        "lent": lent_weights,
    }

    def cover(table, c):
        return next(k for k in table if k[0] <= c[0] and c[1] <= k[1])

    def find(table, c):
        k = cover(table, c)
        return table[k] if k == c else table[k][c[0] - k[0] : c[1] - k[0]]

    queues = {"out": [], "across": [], "in": []}
    queues["out"] += [("out_inner", c, "far_inner", outward) for c in main]
    queues["out"] += [("out_end", c, "far_end", outward) for c in heads + tails]
    queues["across"] += [("far_inner", c, "own", across) for c in main]
    queues["across"] += [("far_end", first, "same", across), ("far_inner", extra, "own", across)]
    queues["across"] += [("far_end", c, "same", across) for c in [extra] + tails]
    queues["in"] += [("same", extra, "own", inward)]
    queues["in"] += [("lent", c, None, inward) for c in pieces]

    arrival = {("own", c): 0 for c in own}
    plan, free, begins = [], dict.fromkeys(queues, 0), {name: [] for name in queues}
    for c in main:
        begin = free["out"]
        arrival["same", c] = free["out"] = free["in"] = begin + c[1] - c[0]
        begins["out"].append(begin)
        begins["in"].append(begin)
        plan.append((("out", "in"), "same", c, "own", swap, begin, free["out"]))
    while any(queues.values()):
        options = []
        for name, queue in queues.items():
            if queue:
                into, c, source, move = queue[0]
                ends = [t for (kind, k), t in arrival.items() if kind == source and k[0] <= c[0] and c[1] <= k[1]]
                if source is None or ends:
                    options.append((max([free[name]] + ends[:1]), name))
        begin, name = min(options)
        into, c, source, move = queues[name].pop(0)
        units = (c[1] - c[0]) * (width // block if source is None else 1)
        free[name] = arrival[into, c] = begin + units
        plan.append(((name,), into, c, source, move, begin, free[name]))

    work = []

    def step(name, c, *needs):
        ready = max(t for need in needs for (kind, k), t in arrival.items() if kind == need and k[0] <= c[0] and c[1] <= k[1])
        work.append((ready, len(work), name, c))

    for c in main:
        step("near", c, "same", "far_inner", "out_inner")
    step("near", extra, "same", "far_inner")
    for c in heads + tails:
        step("far", c, "far_end", "out_end")
    step("far", extra, "far_end")
    for c in pieces:
        step("loan", c, "far_end", "lent")
    work.sort()

    totals = dict.fromkeys(("near", "far", "loan"))

    def run(name, c):
        if name == "near":
            slots = [[own[c]], [same[c]], [far_inner[c]] + ([out_inner[c]] if c in out_inner else [])]
        elif name == "far":
            slots = [[find(far_end, c)] + ([out_end[c]] if c in out_end else [])]
        else:
            slots = [[find(held, c)] for held in (own, far_inner, far_end)]
        weights, offset = (lent_weights[c], jnp.int32(0)) if name == "loan" else (integral, row * ko + c[0])
        totals[name] = contract(slots, weights, offset, totals[name])

    sent = {name: [] for name in queues}
    recent = {name: None for name in totals}
    margin = 2 * (ko // 50 or 1)
    for names, into, c, source, move, begin, end in plan:
        issue = max((sent[n][-1][0] for n in names if sent[n]), default=0)
        while work and work[0][0] + margin <= issue:
            _, _, name, k = work.pop(0)
            run(name, k)
            recent[name] = totals[name]
        if source is None:
            value = lax.dynamic_slice_in_dim(integral, shift + c[0], c[1] - c[0], axis=0)
        else:
            value = find(tables[source], c)
        earlier = [entry[2] for n in queues for entry in [e for e in sent[n] if e[1] <= issue][-1:]]
        earlier += [v for v in recent.values() if v is not None]
        if earlier:
            value = after(value, *earlier)
        tables[into][c] = move(value)
        for n in names:
            sent[n].append((begin, end, tables[into][c]))
    for _, _, name, k in work:
        run(name, k)
    near, far, loan = (totals[name] for name in ("near", "far", "loan"))

    def layer_sum(blocks):
        halves = blocks.reshape(blocks.shape[0], layers, block // layers, width)
        if layers != 2:
            return lax.psum_scatter(halves, "depth", scatter_dimension=1, tiled=False)
        away = lax.dynamic_index_in_dim(halves, 1 - layer, 1, keepdims=False)
        mine = lax.dynamic_index_in_dim(halves, layer, 1, keepdims=False)
        return mine + lax.ppermute(away, "depth", [(0, 1), (1, 0)])

    inner = jnp.logical_or(place == 1, place == 2).astype(jnp.int32)

    def row_sum(halves, swapped):
        def part(target):
            mirrored = jnp.where(place < 2, target, 3 - target)
            slot = mirrored ^ (swapped * (mirrored < 2).astype(jnp.int32))
            return lax.dynamic_index_in_dim(halves, slot, 0, keepdims=False)

        total = part(row)
        for t in range(1, 4):
            total = total + lax.ppermute(part(row ^ t), "row", [(r, r ^ t) for r in range(4)])
        return total

    near = layer_sum(near)
    loan = layer_sum(loan)
    returned = outward(row_sum(jnp.concatenate([jnp.zeros_like(loan[:1]), loan]), 0))
    return row_sum(jnp.concatenate([near, layer_sum(far)]), inner) + returned


def solution(mesh):
    rows, cols, layers = (mesh.shape[name] for name in ("row", "col", "depth"))
    return jax.shard_map(
        lambda amplitude, integral: shards(amplitude, integral, rows, cols, layers),
        mesh=mesh,
        in_specs=(P("row", "depth", "col"), P("depth", None, "col")),
        out_specs=P(("row", "depth"), "col"),
        check_vma=False,
    )
```

```python
import functools

import jax
import jax.numpy as jnp
from jax import lax
from jax.experimental import pallas as pl
from jax.experimental.pallas import tpu as pltpu
from jax.sharding import PartitionSpec as P

LINE = 4
HALVES = 2


def after(value, *earlier):
    return lax.optimization_barrier((value,) + earlier)[0]


def bounds(start, *sizes):
    ends = [start + sum(sizes[: i + 1]) for i in range(len(sizes))]
    return [(stop - size, stop) for stop, size in zip(ends, sizes) if size > 0]


def parts(value):
    high = value.astype(jnp.bfloat16)
    return high, (value - high.astype(jnp.float32)).astype(jnp.bfloat16)


def contract_kernel(terms, per, first, offset_ref, *refs):
    del offset_ref
    out_ref = refs[-1]
    weight_refs = refs[sum(terms) : sum(terms) + per]

    @pl.when(pl.program_id(0) == 0)
    def _():
        out_ref[...] = jnp.zeros_like(out_ref) if first else refs[sum(terms) + per][...]

    left, right = [], []
    for j in range(per):
        highs, lows, at = [], [], 0
        for n in terms:
            value = refs[at][j]
            for ref in refs[at + 1 : at + n]:
                value = value + ref[j]
            at += n
            high, low = parts(value)
            highs.append(high)
            lows.append(low)
        highs = jnp.concatenate(highs, axis=1)
        left += [highs, highs, jnp.concatenate(lows, axis=1)]
        high, low = parts(weight_refs[j][0])
        right += [high, low, high]
    product = lax.dot_general(
        jnp.concatenate(left, axis=0),
        jnp.concatenate(right, axis=0),
        (((0,), (0,)), ((), ())),
        preferred_element_type=jnp.float32,
    )
    out_ref[...] += product.reshape(out_ref.shape)


def contract_run(slots, weights, offset, total, start, per, steps):
    terms = [len(slot) for slot in slots]
    _, depth, block = slots[0][0].shape
    width = weights.shape[2]
    shape = (len(slots), block, width)
    whole = pl.BlockSpec(shape, lambda i, o: (0, 0, 0))
    in_specs = [pl.BlockSpec((per, depth, block), lambda i, o: (start // per + i, 0, 0))] * sum(terms)
    for j in range(per):
        in_specs.append(pl.BlockSpec((1, depth, width), lambda i, o, j=j: (o[0] + start + per * i + j, 0, 0)))
    operands = [a for slot in slots for a in slot] + [weights] * per
    aliases = {}
    if total is not None:
        in_specs.append(whole)
        aliases = {len(operands) + 1: 0}
        operands.append(total)
    return pl.pallas_call(
        functools.partial(contract_kernel, terms, per, total is None),
        out_shape=jax.ShapeDtypeStruct(shape, jnp.float32),
        grid_spec=pltpu.PrefetchScalarGridSpec(
            num_scalar_prefetch=1, grid=(steps,), in_specs=in_specs, out_specs=whole
        ),
        input_output_aliases=aliases,
        compiler_params=pltpu.CompilerParams(vmem_limit_bytes=40 << 20),
    )(jnp.reshape(offset, (1,)).astype(jnp.int32), *operands)


def contract(slots, weights, offset, total):
    count = slots[0][0].shape[0]
    per = max(n for n in range(1, 7) if count % n == 0)
    if per < 3:
        per = min(6, count)
    total = contract_run(slots, weights, offset, total, 0, per, count // per)
    left = count % per
    if left:
        total = contract_run(slots, weights, offset, total, count - left, 1, left)
    return total


def shards(amplitude, integral, rows, cols, layers):
    group = cols // LINE
    row, col, layer = (lax.axis_index(name) for name in ("row", "col", "depth"))
    if group > 1:
        groups = [[z * group + lane for lane in range(group)] for z in range(LINE)]
        amplitude = lax.all_gather(amplitude, "col", axis=2, axis_index_groups=groups, tiled=True)
    place = col // group
    block, width = amplitude.shape[2], integral.shape[2]
    integral = jnp.transpose(integral, (1, 0, 2)).reshape(-1, integral.shape[0] // HALVES, width)
    amplitude = amplitude.reshape(-1, amplitude.shape[1] // HALVES, block)
    ko = amplitude.shape[0]

    def hop(pairs):
        lanes = [(a * group + lane, b * group + lane) for a, b in pairs for lane in range(group)]
        return lambda value: lax.ppermute(value, "col", lanes)

    inward, across, outward = hop([(0, 1), (3, 2)]), hop([(1, 2), (2, 1)]), hop([(1, 0), (2, 3)])
    swap = hop([(0, 1), (1, 0), (2, 3), (3, 2)])

    lent = round(ko * 2 * block / (3 * block + width))
    base = ko - lent
    main = bounds(0, base // 2, base - base // 2)
    extra = (base, ko)
    pieces = bounds(base, *[lent // 5 + (i < lent % 5) for i in range(5)])
    first, second = main
    half = (first[1] - first[0]) // 2
    third = (second[1] - second[0]) // 3
    heads = bounds(first[0], first[1] - first[0] - half, half)
    tails = bounds(second[0], second[1] - second[0] - third, third)

    own = {first: amplitude[: first[1]]}
    later = after(amplitude, own[first])
    shift = after(row, own[first]) * ko
    for c in [second, extra]:
        own[c] = later[c[0] : c[1]]
    same, far_inner, far_end, out_inner, out_end, lent_weights = {}, {}, {}, {}, {}, {}
    tables = {
        "own": own,
        "same": same,
        "far_inner": far_inner,
        "far_end": far_end,
        "out_inner": out_inner,
        "out_end": out_end,
        "lent": lent_weights,
    }

    def cover(table, c):
        return next(k for k in table if k[0] <= c[0] and c[1] <= k[1])

    def find(table, c):
        k = cover(table, c)
        return table[k] if k == c else table[k][c[0] - k[0] : c[1] - k[0]]

    queues = {"out": [], "across": [], "in": []}
    queues["out"] += [("out_inner", c, "far_inner", outward) for c in main]
    queues["out"] += [("out_end", c, "far_end", outward) for c in heads + tails]
    queues["across"] += [("far_inner", c, "own", across) for c in main]
    queues["across"] += [("far_end", first, "same", across), ("far_inner", extra, "own", across)]
    queues["across"] += [("far_end", c, "same", across) for c in [tails[0], extra, tails[1]]]
    queues["in"] += [("same", extra, "own", inward)]
    queues["in"] += [("lent", c, None, inward) for c in pieces]

    arrival = {("own", c): 0 for c in own}
    plan, free, begins = [], dict.fromkeys(queues, 0), {name: [] for name in queues}
    for c in main:
        begin = free["out"]
        arrival["same", c] = free["out"] = free["in"] = begin + c[1] - c[0]
        begins["out"].append(begin)
        begins["in"].append(begin)
        plan.append((("out", "in"), "same", c, "own", swap, begin, free["out"]))
    while any(queues.values()):
        options = []
        for name, queue in queues.items():
            if queue:
                into, c, source, move = queue[0]
                ends = [t for (kind, k), t in arrival.items() if kind == source and k[0] <= c[0] and c[1] <= k[1]]
                if source is None or ends:
                    options.append((max([free[name]] + ends[:1]), name))
        begin, name = min(options)
        into, c, source, move = queues[name].pop(0)
        units = (c[1] - c[0]) * (width // block if source is None else 1)
        free[name] = arrival[into, c] = begin + units
        plan.append(((name,), into, c, source, move, begin, free[name]))

    work = []

    def step(name, c, *needs):
        ready = max(t for need in needs for (kind, k), t in arrival.items() if kind == need and k[0] <= c[0] and c[1] <= k[1])
        work.append((ready, len(work), name, c))

    for c in main:
        step("near", c, "same", "far_inner", "out_inner")
    step("near", extra, "same", "far_inner")
    for c in heads + tails:
        step("far", c, "far_end", "out_end")
    step("far", extra, "far_end")
    for c in pieces:
        step("loan", c, "far_end", "lent")
    work.sort()

    totals = dict.fromkeys(("near", "far", "loan"))

    def run(name, c):
        if name == "near":
            slots = [[own[c]], [same[c]], [far_inner[c]] + ([out_inner[c]] if c in out_inner else [])]
        elif name == "far":
            slots = [[find(far_end, c)] + ([out_end[c]] if c in out_end else [])]
        else:
            slots = [[find(held, c)] for held in (own, far_inner, far_end)]
        weights, offset = (lent_weights[c], jnp.int32(0)) if name == "loan" else (integral, row * ko + c[0])
        totals[name] = contract(slots, weights, offset, totals[name])

    sent = {name: [] for name in queues}
    recent = {name: None for name in totals}
    margin = 2 * (ko // 50 or 1)
    for names, into, c, source, move, begin, end in plan:
        issue = max((sent[n][-1][0] for n in names if sent[n]), default=0)
        while work and work[0][0] + margin <= issue:
            _, _, name, k = work.pop(0)
            run(name, k)
            recent[name] = totals[name]
        if source is None:
            value = lax.dynamic_slice_in_dim(integral, shift + c[0], c[1] - c[0], axis=0)
        else:
            value = find(tables[source], c)
        earlier = [entry[2] for n in queues for entry in [e for e in sent[n] if e[1] <= issue][-1:]]
        earlier += [v for v in recent.values() if v is not None]
        if earlier:
            value = after(value, *earlier)
        tables[into][c] = move(value)
        for n in names:
            sent[n].append((begin, end, tables[into][c]))
    def layer_sum(blocks):
        halves = blocks.reshape(blocks.shape[0], layers, block // layers, width)
        if layers != 2:
            return lax.psum_scatter(halves, "depth", scatter_dimension=1, tiled=False)
        away = lax.dynamic_index_in_dim(halves, 1 - layer, 1, keepdims=False)
        mine = lax.dynamic_index_in_dim(halves, layer, 1, keepdims=False)
        return mine + lax.ppermute(away, "depth", [(0, 1), (1, 0)])

    inner = jnp.logical_or(place == 1, place == 2).astype(jnp.int32)

    def row_sum(halves, swapped):
        def part(target):
            mirrored = jnp.where(place < 2, target, 3 - target)
            slot = mirrored ^ (swapped * (mirrored < 2).astype(jnp.int32))
            return lax.dynamic_index_in_dim(halves, slot, 0, keepdims=False)

        total = part(row)
        for t in range(1, 4):
            total = total + lax.ppermute(part(row ^ t), "row", [(r, r ^ t) for r in range(4)])
        return total

    last = ("far", tails[1])
    for _, _, name, k in work:
        if (name, k) != last:
            run(name, k)
    near = layer_sum(totals["near"])
    loan = layer_sum(totals["loan"])
    run(*last)
    returned = outward(row_sum(jnp.concatenate([jnp.zeros_like(loan[:1]), loan]), 0))
    return row_sum(jnp.concatenate([near, layer_sum(totals["far"])]), inner) + returned


def solution(mesh):
    rows, cols, layers = (mesh.shape[name] for name in ("row", "col", "depth"))
    return jax.shard_map(
        lambda amplitude, integral: shards(amplitude, integral, rows, cols, layers),
        mesh=mesh,
        in_specs=(P("row", "depth", "col"), P("depth", None, "col")),
        out_specs=P(("row", "depth"), "col"),
        check_vma=False,
    )
```

```python
import functools

import jax
import jax.numpy as jnp
from jax import lax
from jax.experimental import pallas as pl
from jax.experimental.pallas import tpu as pltpu
from jax.sharding import PartitionSpec as P

LINE = 4
HALVES = 2


def after(value, *earlier):
    return lax.optimization_barrier((value,) + earlier)[0]


def bounds(start, *sizes):
    ends = [start + sum(sizes[: i + 1]) for i in range(len(sizes))]
    return [(stop - size, stop) for stop, size in zip(ends, sizes) if size > 0]


def parts(value):
    high = value.astype(jnp.bfloat16)
    return high, (value - high.astype(jnp.float32)).astype(jnp.bfloat16)


def contract_kernel(terms, per, first, offset_ref, *refs):
    del offset_ref
    out_ref = refs[-1]
    weight_refs = refs[sum(terms) : sum(terms) + per]

    @pl.when(pl.program_id(0) == 0)
    def _():
        out_ref[...] = jnp.zeros_like(out_ref) if first else refs[sum(terms) + per][...]

    left, right = [], []
    for j in range(per):
        highs, lows, at = [], [], 0
        for n in terms:
            value = refs[at][j]
            for ref in refs[at + 1 : at + n]:
                value = value + ref[j]
            at += n
            high, low = parts(value)
            highs.append(high)
            lows.append(low)
        highs = jnp.concatenate(highs, axis=1)
        left += [highs, highs, jnp.concatenate(lows, axis=1)]
        high, low = parts(weight_refs[j][0])
        right += [high, low, high]
    product = lax.dot_general(
        jnp.concatenate(left, axis=0),
        jnp.concatenate(right, axis=0),
        (((0,), (0,)), ((), ())),
        preferred_element_type=jnp.float32,
    )
    out_ref[...] += product.reshape(out_ref.shape)


def contract_run(slots, weights, offset, total, start, per, steps):
    terms = [len(slot) for slot in slots]
    _, depth, block = slots[0][0].shape
    width = weights.shape[2]
    shape = (len(slots), block, width)
    whole = pl.BlockSpec(shape, lambda i, o: (0, 0, 0))
    in_specs = [pl.BlockSpec((per, depth, block), lambda i, o: (start // per + i, 0, 0))] * sum(terms)
    for j in range(per):
        in_specs.append(pl.BlockSpec((1, depth, width), lambda i, o, j=j: (o[0] + start + per * i + j, 0, 0)))
    operands = [a for slot in slots for a in slot] + [weights] * per
    aliases = {}
    if total is not None:
        in_specs.append(whole)
        aliases = {len(operands) + 1: 0}
        operands.append(total)
    return pl.pallas_call(
        functools.partial(contract_kernel, terms, per, total is None),
        out_shape=jax.ShapeDtypeStruct(shape, jnp.float32),
        grid_spec=pltpu.PrefetchScalarGridSpec(
            num_scalar_prefetch=1, grid=(steps,), in_specs=in_specs, out_specs=whole
        ),
        input_output_aliases=aliases,
        compiler_params=pltpu.CompilerParams(vmem_limit_bytes=40 << 20),
    )(jnp.reshape(offset, (1,)).astype(jnp.int32), *operands)


def contract(slots, weights, offset, total):
    count = slots[0][0].shape[0]
    per = max(n for n in range(1, 7) if count % n == 0)
    if per < 3:
        per = min(6, count)
    total = contract_run(slots, weights, offset, total, 0, per, count // per)
    left = count % per
    if left:
        total = contract_run(slots, weights, offset, total, count - left, 1, left)
    return total


def shards(amplitude, integral, rows, cols, layers):
    group = cols // LINE
    row, col, layer = (lax.axis_index(name) for name in ("row", "col", "depth"))
    if group > 1:
        groups = [[z * group + lane for lane in range(group)] for z in range(LINE)]
        amplitude = lax.all_gather(amplitude, "col", axis=2, axis_index_groups=groups, tiled=True)
    place = col // group
    block, width = amplitude.shape[2], integral.shape[2]
    integral = jnp.transpose(integral, (1, 0, 2)).reshape(-1, integral.shape[0] // HALVES, width)
    amplitude = amplitude.reshape(-1, amplitude.shape[1] // HALVES, block)
    ko = amplitude.shape[0]

    def hop(pairs):
        lanes = [(a * group + lane, b * group + lane) for a, b in pairs for lane in range(group)]
        return lambda value: lax.ppermute(value, "col", lanes)

    inward, across, outward = hop([(0, 1), (3, 2)]), hop([(1, 2), (2, 1)]), hop([(1, 0), (2, 3)])
    swap = hop([(0, 1), (1, 0), (2, 3), (3, 2)])

    lent = round(ko * 2 * block / (3 * block + width))
    base = ko - lent
    main = bounds(0, base // 2, base - base // 2)
    extra = (base, ko)
    pieces = bounds(base, *[lent // 5 + (i < lent % 5) for i in range(5)])
    first, second = main
    half = (first[1] - first[0]) // 2
    third = (second[1] - second[0]) // 3
    heads = bounds(first[0], first[1] - first[0] - half, half)
    tails = bounds(second[0], second[1] - second[0] - third, third)

    own = {first: amplitude[: first[1]]}
    later = after(amplitude, own[first])
    shift = after(row, own[first]) * ko
    for c in [second, extra]:
        own[c] = later[c[0] : c[1]]
    same, far_inner, far_end, out_inner, out_end, lent_weights = {}, {}, {}, {}, {}, {}
    tables = {
        "own": own,
        "same": same,
        "far_inner": far_inner,
        "far_end": far_end,
        "out_inner": out_inner,
        "out_end": out_end,
        "lent": lent_weights,
    }

    def cover(table, c):
        return next(k for k in table if k[0] <= c[0] and c[1] <= k[1])

    def find(table, c):
        k = cover(table, c)
        return table[k] if k == c else table[k][c[0] - k[0] : c[1] - k[0]]

    queues = {"out": [], "across": [], "in": []}
    queues["out"] += [("out_inner", c, "far_inner", outward) for c in main]
    queues["out"] += [("out_end", c, "far_end", outward) for c in heads + tails]
    queues["across"] += [("far_inner", c, "own", across) for c in main]
    queues["across"] += [("far_end", first, "same", across), ("far_inner", extra, "own", across)]
    queues["across"] += [("far_end", c, "same", across) for c in [tails[0], extra, tails[1]]]
    queues["in"] += [("same", extra, "own", inward)]
    queues["in"] += [("lent", c, None, inward) for c in pieces]

    arrival = {("own", c): 0 for c in own}
    plan, free, begins = [], dict.fromkeys(queues, 0), {name: [] for name in queues}
    for c in main:
        begin = free["out"]
        arrival["same", c] = free["out"] = free["in"] = begin + c[1] - c[0]
        begins["out"].append(begin)
        begins["in"].append(begin)
        plan.append((("out", "in"), "same", c, "own", swap, begin, free["out"]))
    while any(queues.values()):
        options = []
        for name, queue in queues.items():
            if queue:
                into, c, source, move = queue[0]
                ends = [t for (kind, k), t in arrival.items() if kind == source and k[0] <= c[0] and c[1] <= k[1]]
                if source is None or ends:
                    options.append((max([free[name]] + ends[:1]), name))
        begin, name = min(options)
        into, c, source, move = queues[name].pop(0)
        units = (c[1] - c[0]) * (width // block if source is None else 1)
        free[name] = arrival[into, c] = begin + units
        plan.append(((name,), into, c, source, move, begin, free[name]))

    work = []

    def step(name, c, *needs):
        ready = max(t for need in needs for (kind, k), t in arrival.items() if kind == need and k[0] <= c[0] and c[1] <= k[1])
        work.append((ready, len(work), name, c))

    for c in main:
        step("near", c, "same", "far_inner", "out_inner")
    step("near", extra, "same", "far_inner")
    for c in heads + tails:
        step("far", c, "far_end", "out_end")
    step("far", extra, "far_end")
    for c in pieces:
        step("loan", c, "far_end", "lent")
    work.sort()

    totals = dict.fromkeys(("near", "far", "loan"))

    def run(name, c):
        if name == "near":
            slots = [[own[c]], [same[c]], [far_inner[c]] + ([out_inner[c]] if c in out_inner else [])]
        elif name == "far":
            slots = [[find(far_end, c)] + ([out_end[c]] if c in out_end else [])]
        else:
            slots = [[find(held, c)] for held in (own, far_inner, far_end)]
        weights, offset = (lent_weights[c], jnp.int32(0)) if name == "loan" else (integral, row * ko + c[0])
        totals[name] = contract(slots, weights, offset, totals[name])

    sent = {name: [] for name in queues}
    recent = {name: None for name in totals}
    margin = 2 * (ko // 50 or 1)
    for names, into, c, source, move, begin, end in plan:
        issue = max((sent[n][-1][0] for n in names if sent[n]), default=0)
        while work and work[0][0] + margin <= issue:
            _, _, name, k = work.pop(0)
            run(name, k)
            recent[name] = totals[name]
        if source is None:
            value = lax.dynamic_slice_in_dim(integral, shift + c[0], c[1] - c[0], axis=0)
        else:
            value = find(tables[source], c)
        earlier = [entry[2] for n in queues for entry in [e for e in sent[n] if e[1] <= issue][-1:]]
        earlier += [v for v in recent.values() if v is not None]
        if (into, c) == ("far_end", extra):
            earlier.append(far_end[tails[0]])
        if earlier:
            value = after(value, *earlier)
        tables[into][c] = move(value)
        for n in names:
            sent[n].append((begin, end, tables[into][c]))
    def layer_sum(blocks):
        halves = blocks.reshape(blocks.shape[0], layers, block // layers, width)
        if layers != 2:
            return lax.psum_scatter(halves, "depth", scatter_dimension=1, tiled=False)
        away = lax.dynamic_index_in_dim(halves, 1 - layer, 1, keepdims=False)
        mine = lax.dynamic_index_in_dim(halves, layer, 1, keepdims=False)
        return mine + lax.ppermute(away, "depth", [(0, 1), (1, 0)])

    inner = jnp.logical_or(place == 1, place == 2).astype(jnp.int32)

    def row_sum(halves, swapped):
        def part(target):
            mirrored = jnp.where(place < 2, target, 3 - target)
            slot = mirrored ^ (swapped * (mirrored < 2).astype(jnp.int32))
            return lax.dynamic_index_in_dim(halves, slot, 0, keepdims=False)

        total = part(row)
        for t in range(1, 4):
            total = total + lax.ppermute(part(row ^ t), "row", [(r, r ^ t) for r in range(4)])
        return total

    last = ("far", tails[1])
    for _, _, name, k in work:
        if (name, k) != last:
            run(name, k)
    near = layer_sum(totals["near"])
    loan = layer_sum(totals["loan"])
    run(*last)
    returned = outward(row_sum(jnp.concatenate([jnp.zeros_like(loan[:1]), loan]), 0))
    return row_sum(jnp.concatenate([near, layer_sum(totals["far"])]), inner) + returned


def solution(mesh):
    rows, cols, layers = (mesh.shape[name] for name in ("row", "col", "depth"))
    return jax.shard_map(
        lambda amplitude, integral: shards(amplitude, integral, rows, cols, layers),
        mesh=mesh,
        in_specs=(P("row", "depth", "col"), P("depth", None, "col")),
        out_specs=P(("row", "depth"), "col"),
        check_vma=False,
    )
```
